768 devices in a mesh: dp: 32 (over x_hi, y, core), tensor: 24 (over x_lo, z).
Axes of the slice: x: 4 (x_hi: 2, x_lo: 2; x = x_hi * 2 + x_lo), y: 8, z: 12, core: 2. Of those that a mesh axis runs over, the one named last changes fastest.
Arguments:
- tokens: bfloat16 [4608, 6144], P(('dp', 'tensor')), may hold values from -24 to 24
- norm_gain: float32 [6144], replicated, may hold values from 0.5 to 2
- proj_weight: bfloat16 [6144, 6144], P(None, 'tensor'), may hold values from -0.078125 to 0.078125
- cotangent: bfloat16 [4608, 6144], P('dp', 'tensor'), may hold values from -6 to 6
Outputs:
- projected: bfloat16 [4608, 6144], P('dp', 'tensor')
- input_grad: bfloat16 [4608, 6144], P(('dp', 'tensor'))
- weight_grad: float32 [6144, 6144], P('dp', 'tensor')
- gain_grad: float32 [6144], replicated
The draws below stay inside these ranges and needn't reach their ends.
All inputs are finite; a program needn't handle non-finite values.
Results may differ from the reference program's by a relative error of at most 0.024.
Values may be sent and summed in bfloat16 or wider, within the bound.
No kernel may reach another device: no remote copies, remote signals or barrier semaphores. Data moves between devices by JAX's collectives and lax.ppermute only.
A program may use at most 32 MiB of HBM per device.

```python
import math
import jax
import jax.numpy as jnp
from jax import lax

D = 6144
TOK_DEV = 6
COLS = 6144
TOKENS = 4608
N_DP = 32
N_TENSOR = 24


def raised(result, own_key, source, target, parts, factor):
    owner, partner = [(jnp.arange(result.shape[position]) // (result.shape[position] // parts)).reshape([-1 if axis == position else 1 for axis in range(result.ndim)]) for position in (source, target)]
    chosen = jax.random.permutation(own_key, parts)[partner]
    strong = (owner == chosen) | (owner == (partner + parts // 2) % parts)
    return jnp.where(strong, factor * result, result)


def levels(stream_key, dims, pieces, smallest, largest):
    level, own = 1.0, jax.random.fold_in(stream_key, 6)
    for position, shards_of in pieces:
        draws = jnp.exp(jax.random.uniform(jax.random.fold_in(own, position), (shards_of,), jnp.float32, smallest / len(pieces), largest / len(pieces)))
        level = level * jnp.repeat(draws, dims[position] // shards_of).reshape([-1 if axis == position else 1 for axis in range(len(dims))])
    return level


def bell_draw(rng, extent, deviation, most, cuts=(), kind=jnp.bfloat16):
    array = deviation * jax.random.normal(rng, extent, jnp.float32)
    if cuts:
        array = array * levels(rng, extent, cuts, -0.22, 0.18)
    return jnp.clip(array, -most, most).astype(kind)


def gaussian_with(key, extent, spread, limit, shards, heavy, dtype=jnp.bfloat16):
    entries = spread * jax.random.normal(key, extent, jnp.float32)
    if shards:
        entries = entries * levels(key, extent, shards, -0.22, 0.18)
    return jnp.clip(raised(entries, jax.random.fold_in(key, 3), *heavy), -limit, limit).astype(dtype)


def setup_inputs(seed: int = 0) -> dict:
    seeds = jax.random.split(jax.random.key(seed), 5)
    return {
        "tokens": gaussian_with(seeds[0], (TOKENS, D), 1.0, 24.0, ((0, 768),), (0, 1, 768, 6.0)),
        "norm_gain": jnp.clip(jnp.exp(jax.random.uniform(seeds[1], (D,), jnp.float32, math.log(0.5), math.log(2.0))), 0.5, 2.0),
        "proj_weight": bell_draw(seeds[2], (D, COLS), D ** -0.5, 0.078125, ((1, 24),)),
        "cotangent": bell_draw(seeds[3], (TOKENS, COLS), 1.0, 6.0, ((0, 32), (1, 24))),
    }


def normalize(tokens, norm_gain):
    values = tokens.astype(jnp.float32)
    inverse = lax.rsqrt(lax.optimization_barrier(jnp.mean(values * values, axis=-1, keepdims=True)) + 1e-05)
    unit_rows = values * inverse
    return (inverse, unit_rows, unit_rows * norm_gain)

def restore_rows(normed):
    blocks = normed.reshape(normed.shape[0], normed.shape[1] // 128, 128)
    scales = (lax.optimization_barrier(jnp.max(jnp.abs(blocks), axis=-1)) + 1e-06) / 448.0
    payload = (blocks / scales[..., None]).astype(jnp.bfloat16)
    return (payload.astype(jnp.float32) * scales[..., None]).reshape(normed.shape).astype(jnp.bfloat16)

def reference(tokens, norm_gain, proj_weight, cotangent):
    inverse, unit_rows, normed = normalize(tokens, norm_gain)
    restored = restore_rows(normed)
    projected = jnp.dot(restored, proj_weight, preferred_element_type=jnp.float32).astype(jnp.bfloat16)
    block_cols = COLS // N_TENSOR

    def input_step(index, total):
        offset = (index * block_cols).astype(jnp.int32)
        weight_block = lax.dynamic_slice_in_dim(proj_weight, offset, block_cols, 1)
        grad_block = lax.dynamic_slice_in_dim(cotangent, offset, block_cols, 1)
        term = lax.dot_general(grad_block, weight_block, (((1,), (1,)), ((), ())), preferred_element_type=jnp.float32)
        return total + term.astype(jnp.bfloat16).astype(jnp.float32)
    normed_grad = lax.fori_loop(0, N_TENSOR, input_step, jnp.zeros((TOKENS, D), jnp.float32))
    group_rows = TOK_DEV * N_TENSOR

    def weight_step(index, total):
        offset = (index * group_rows).astype(jnp.int32)
        rows_in = lax.dynamic_slice_in_dim(restored, offset, group_rows, 0)
        rows_grad = lax.dynamic_slice_in_dim(cotangent, offset, group_rows, 0)
        term = lax.dot_general(rows_in, rows_grad, (((0,), (0,)), ((), ())), preferred_element_type=jnp.float32)
        return total + term.astype(jnp.bfloat16).astype(jnp.float32)
    weight_grad = lax.fori_loop(0, N_DP, weight_step, jnp.zeros((D, COLS), jnp.float32))
    gain_grad = lax.optimization_barrier(jnp.sum(normed_grad * unit_rows, axis=0))
    scaled = normed_grad * norm_gain
    input_grad = (inverse * (scaled - unit_rows * lax.optimization_barrier(jnp.mean(scaled * unit_rows, axis=-1, keepdims=True)))).astype(jnp.bfloat16)
    return (projected, input_grad, weight_grad, gain_grad)
```

```python
import jax
import jax.numpy as jnp
from jax import lax
from jax.experimental import pallas as pl
from jax.experimental.pallas import tpu as pltpu
from jax.sharding import Mesh, PartitionSpec as P

XH, Y, CORE, XL, Z = 2, 8, 2, 2, 12
AXES = ("xh", "y", "c", "xl", "z")
DP, TENSOR = ("xh", "y", "c"), ("xl", "z")
TOK, D, COLS = 6, 6144, 256
Q, FQ = 4, 1536
GROUP = TOK * XL * Z
ROWS = GROUP * Q
BLOCK = 384
NT = (((1,), (1,)), ((), ()))
TN = (((0,), (0,)), ((), ()))


def grad_kernel(cot_ref, w_ref, term_ref, comm_ref, wide):
    for q in range(Q):
        part = lax.dot_general(
            cot_ref[...],
            w_ref[q * FQ : (q + 1) * FQ, :],
            NT,
            preferred_element_type=jnp.float32,
        )
        term_ref[:, q * FQ : (q + 1) * FQ] = part.astype(jnp.bfloat16)
        for b in range(FQ // 128):
            wide[b, pl.ds(q, GROUP, stride=Q), :] = part[:, b * 128 : (b + 1) * 128]
    for b in range(FQ // 128):
        comm_ref[:, b * 128 : (b + 1) * 128] = wide[b].astype(jnp.bfloat16)


def grad_terms(cotangent, weight):
    vmem = pl.BlockSpec(memory_space=pltpu.VMEM)
    return pl.pallas_call(
        grad_kernel,
        out_shape=(
            jax.ShapeDtypeStruct((GROUP, D), jnp.bfloat16),
            jax.ShapeDtypeStruct((ROWS, FQ), jnp.bfloat16),
        ),
        in_specs=[vmem] * 2,
        out_specs=(vmem, vmem),
        scratch_shapes=[pltpu.VMEM((FQ // 128, ROWS, 128), jnp.float32)],
        compiler_params=pltpu.CompilerParams(vmem_limit_bytes=40 * 2**20),
        cost_estimate=pl.CostEstimate(
            flops=2 * GROUP * D * COLS, bytes_accessed=7 * 2**20, transcendentals=0
        ),
    )(cotangent, weight)


def main_kernel(
    side_ref, own_ref, other_ref, w_ref, cot_ref, gain_ref, term_ref,
    proj_ref, wgrad_ref, part_ref, wide,
):
    half = ROWS // 2
    mine = pl.multiple_of(side_ref[0] * half, half)
    theirs = pl.multiple_of((1 - side_ref[0]) * half, half)
    for b in range(FQ // 128):
        wide[b, pl.ds(mine, half), :] = own_ref[:, b * 128 : (b + 1) * 128].astype(jnp.float32)
        wide[b, pl.ds(theirs, half), :] = other_ref[:, b * 128 : (b + 1) * 128].astype(jnp.float32)
    squares = jnp.zeros((GROUP, 128), jnp.float32)
    for b in range(FQ // 128):
        for q in range(Q):
            values = wide[b, pl.ds(q, GROUP, stride=Q), :]
            squares += values * values
    inverse = lax.rsqrt(jnp.sum(squares, axis=1, keepdims=True) / D + 1e-05)
    total = jnp.zeros((GROUP, COLS), jnp.float32)
    for p in range(D // BLOCK):
        q, first = divmod(p * BLOCK, FQ)
        pieces = []
        for b in range(BLOCK // 128):
            at = p * BLOCK + b * 128
            unit = wide[first // 128 + b, pl.ds(q, GROUP, stride=Q), :] * inverse
            part_ref[:, at : at + 128] = jnp.sum(
                unit * term_ref[:, at : at + 128].astype(jnp.float32), axis=0, keepdims=True
            )
            normed = unit * gain_ref[:, at : at + 128]
            scale = (jnp.max(jnp.abs(normed), axis=1, keepdims=True) + 1e-06) / 448.0
            payload = (normed / scale).astype(jnp.bfloat16)
            pieces.append((payload.astype(jnp.float32) * scale).astype(jnp.bfloat16))
        restored = jnp.concatenate(pieces, axis=1)
        total += jnp.dot(
            restored, w_ref[p * BLOCK : (p + 1) * BLOCK, :], preferred_element_type=jnp.float32
        )
        product = lax.dot_general(
            restored, cot_ref[...], TN, preferred_element_type=jnp.float32
        ).astype(jnp.bfloat16)
        wgrad_ref[0, p] = product[: BLOCK // 2]
        wgrad_ref[1, p] = product[BLOCK // 2 :]
    proj_ref[...] = total.astype(jnp.bfloat16)


def main_products(side, own, other, weight, cotangent, gain, term):
    vmem = pl.BlockSpec(memory_space=pltpu.VMEM)
    return pl.pallas_call(
        main_kernel,
        out_shape=(
            jax.ShapeDtypeStruct((GROUP, COLS), jnp.bfloat16),
            jax.ShapeDtypeStruct((CORE, XH * Y, BLOCK // 2, COLS), jnp.bfloat16),
            jax.ShapeDtypeStruct((1, D), jnp.float32),
        ),
        in_specs=[pl.BlockSpec(memory_space=pltpu.SMEM)] + [vmem] * 6,
        out_specs=(vmem, vmem, vmem),
        scratch_shapes=[pltpu.VMEM((FQ // 128, ROWS, 128), jnp.float32)],
        compiler_params=pltpu.CompilerParams(vmem_limit_bytes=40 * 2**20),
        cost_estimate=pl.CostEstimate(
            flops=4 * GROUP * D * COLS, bytes_accessed=12 * 2**20, transcendentals=0
        ),
    )(side, own, other, weight, cotangent, gain, term)


def exchange(array, axes):
    return lax.all_to_all(array, axes, 0, 0, tiled=True)


def body(tokens, norm_gain, proj_weight, cotangent):
    term, comm = grad_terms(cotangent, proj_weight)
    grad_rows = lax.psum_scatter(comm, TENSOR, scatter_dimension=0, tiled=True)

    chunk = tokens.reshape(TOK * Q, FQ)
    own = lax.all_gather(chunk, "z", axis=0, tiled=True)
    other = lax.ppermute(own, "xl", [(0, 1), (1, 0)])
    side = lax.axis_index("xl").astype(jnp.int32).reshape(1)
    projected, wgrad, part = main_products(
        side, own, other, proj_weight, cotangent, norm_gain.reshape(1, D), term
    )

    wgrad = exchange(wgrad, "c").astype(jnp.float32)
    wgrad = (wgrad[0] + wgrad[1]).astype(jnp.bfloat16)
    wgrad = exchange(wgrad, ("xh", "y"))
    weight_grad = jnp.sum(wgrad.astype(jnp.float32), axis=0)

    slots = XL * Z
    part = exchange(part.reshape(slots, D // slots), TENSOR)
    part = jnp.sum(part, axis=0)
    part = exchange(jnp.broadcast_to(part, (XH * Y * CORE, D // slots)), DP)
    part = jnp.sum(part, axis=0)
    part = exchange(jnp.broadcast_to(part, (slots, D // slots)), TENSOR)
    gain_grad = part.reshape(D)

    values = tokens.astype(jnp.float32)
    inverse = lax.rsqrt(jnp.mean(values * values, axis=-1, keepdims=True) + 1e-05)
    unit_rows = values * inverse
    normed_grad = grad_rows.reshape(TOK, D).astype(jnp.float32)
    scaled = normed_grad * norm_gain
    input_grad = (
        inverse * (scaled - unit_rows * jnp.mean(scaled * unit_rows, axis=-1, keepdims=True))
    ).astype(jnp.bfloat16)
    return projected, input_grad, weight_grad, gain_grad


def solution(mesh):
    fine = Mesh(mesh.devices.reshape(XH, Y, CORE, XL, Z), AXES)
    return jax.shard_map(
        body,
        mesh=fine,
        in_specs=(P(DP + TENSOR, None), P(), P(None, TENSOR), P(DP, TENSOR)),
        out_specs=(P(DP, TENSOR), P(DP + TENSOR, None), P(DP, TENSOR), P()),
        check_vma=False,
    )
```

```python
import jax
import jax.numpy as jnp
from jax import lax
from jax.experimental import pallas as pl
from jax.experimental.pallas import tpu as pltpu
from jax.sharding import Mesh, PartitionSpec as P

XH, Y, CORE, XL, Z = 2, 8, 2, 2, 12
AXES = ("xh", "y", "c", "xl", "z")
DP, TENSOR = ("xh", "y", "c"), ("xl", "z")
TOK, D, COLS = 6, 6144, 256
Q, FQ = 4, 1536
GROUP = TOK * XL * Z
ROWS = GROUP * Q
HALF = ROWS // 2
CHUNK = TOK * Q
BLOCK = 384
OWNED = BLOCK // 2
NT = (((1,), (1,)), ((), ()))
TN = (((0,), (0,)), ((), ()))
VMEM = pl.BlockSpec(memory_space=pltpu.VMEM)
SMEM = pl.BlockSpec(memory_space=pltpu.SMEM)
PARAMS = pltpu.CompilerParams(vmem_limit_bytes=40 * 2**20)


def grad_kernel(side_ref, cot_ref, w_ref, comm_ref, keep_ref, send_ref, wide):
    mine = pl.multiple_of(side_ref[0] * HALF, HALF)
    theirs = pl.multiple_of((1 - side_ref[0]) * HALF, HALF)
    for q in range(Q):
        part = lax.dot_general(cot_ref[...], w_ref[q], NT, preferred_element_type=jnp.float32)
        for b in range(BLOCK // 128):
            wide[b, pl.ds(q, GROUP, stride=Q), :] = part[:, b * 128 : (b + 1) * 128]
    for b in range(BLOCK // 128):
        lanes = slice(b * 128, (b + 1) * 128)
        keep_ref[:, lanes] = wide[b, pl.ds(mine, HALF), :].astype(jnp.bfloat16)
        send_ref[:, lanes] = wide[b, pl.ds(theirs, HALF), :].astype(jnp.bfloat16)
        starts = [x * HALF + z * CHUNK for z in range(Z) for x in range(XL)]
        ordered = jnp.concatenate([wide[b, start : start + CHUNK, :] for start in starts])
        comm_ref[:, lanes] = ordered.astype(jnp.bfloat16)


def grad_terms(side, cotangent, weight):
    half = jax.ShapeDtypeStruct((HALF, FQ), jnp.bfloat16)
    return pl.pallas_call(
        grad_kernel,
        grid=(FQ // BLOCK,),
        out_shape=(jax.ShapeDtypeStruct((ROWS, FQ), jnp.bfloat16), half, half),
        in_specs=[
            SMEM,
            pl.BlockSpec((GROUP, COLS), lambda i: (0, 0)),
            pl.BlockSpec((Q, BLOCK, COLS), lambda i: (0, i, 0)),
        ],
        out_specs=(
            pl.BlockSpec((ROWS, BLOCK), lambda i: (0, i)),
            pl.BlockSpec((HALF, BLOCK), lambda i: (0, i)),
            pl.BlockSpec((HALF, BLOCK), lambda i: (0, i)),
        ),
        scratch_shapes=[pltpu.VMEM((BLOCK // 128, ROWS, 128), jnp.float32)],
        compiler_params=PARAMS,
        cost_estimate=pl.CostEstimate(
            flops=2 * GROUP * D * COLS, bytes_accessed=5 * 2**20, transcendentals=0
        ),
    )(side, cotangent, weight.reshape(Q, FQ, COLS))


def row_inverse(squares, rows, tokens):
    rows[...] = squares
    total = jnp.zeros((tokens, 128), jnp.float32)
    for q in range(Q):
        total += rows[pl.ds(q, tokens, stride=Q), :]
    return lax.rsqrt(jnp.sum(total, axis=1, keepdims=True) / D + 1e-05)


def gain_kernel(own_ref, keep_ref, got_ref, part_ref, rows):
    squares = jnp.zeros((HALF, 128), jnp.float32)
    for b in range(FQ // 128):
        values = own_ref[:, b * 128 : (b + 1) * 128].astype(jnp.float32)
        squares += values * values
    inverse = row_inverse(squares, rows, GROUP // 2)
    for q in range(Q):
        rows[pl.ds(q, GROUP // 2, stride=Q), :] = jnp.broadcast_to(inverse, (GROUP // 2, 128))
    for b in range(FQ // 128):
        lanes = slice(b * 128, (b + 1) * 128)
        term = keep_ref[:, lanes].astype(jnp.float32) + got_ref[:, lanes].astype(jnp.float32)
        product = own_ref[:, lanes].astype(jnp.float32) * rows[...] * term
        total = jnp.sum(product.reshape(HALF // 8, 8, 128), axis=0)
        part_ref[:, lanes] = total[:Q] + total[Q:]


def gain_terms(own, keep, got):
    return pl.pallas_call(
        gain_kernel,
        out_shape=jax.ShapeDtypeStruct((Q, FQ), jnp.float32),
        in_specs=[VMEM] * 3,
        out_specs=VMEM,
        scratch_shapes=[pltpu.VMEM((HALF, 128), jnp.float32)],
        compiler_params=PARAMS,
        cost_estimate=pl.CostEstimate(flops=5 * 2**20, bytes_accessed=4 * 2**20, transcendentals=0),
    )(own, keep, got)


def main_kernel(
    side_ref, own_ref, other_ref, w_ref, cot_ref, gain_ref,
    proj_ref, keep_ref, send_ref, wide, rows,
):
    mine = pl.multiple_of(side_ref[0] * HALF, HALF)
    theirs = pl.multiple_of((1 - side_ref[0]) * HALF, HALF)
    for b in range(FQ // 128):
        wide[b, pl.ds(mine, HALF), :] = own_ref[:, b * 128 : (b + 1) * 128].astype(jnp.float32)
        wide[b, pl.ds(theirs, HALF), :] = other_ref[:, b * 128 : (b + 1) * 128].astype(jnp.float32)
    squares = jnp.zeros((ROWS, 128), jnp.float32)
    for b in range(FQ // 128):
        squares += wide[b] * wide[b]
    inverse = row_inverse(squares, rows, GROUP)
    total = jnp.zeros((GROUP, COLS), jnp.float32)
    for p in range(D // BLOCK):
        q, first = divmod(p * BLOCK, FQ)
        pieces = []
        for b in range(BLOCK // 128):
            at = p * BLOCK + b * 128
            unit = wide[first // 128 + b, pl.ds(q, GROUP, stride=Q), :] * inverse
            normed = unit * gain_ref[:, at : at + 128]
            scale = (jnp.max(jnp.abs(normed), axis=1, keepdims=True) + 1e-06) / 448.0
            payload = (normed / scale).astype(jnp.bfloat16)
            pieces.append((payload.astype(jnp.float32) * scale).astype(jnp.bfloat16))
        restored = jnp.concatenate(pieces, axis=1)
        total += jnp.dot(
            restored, w_ref[p * BLOCK : (p + 1) * BLOCK, :], preferred_element_type=jnp.float32
        )
        product = lax.dot_general(
            restored, cot_ref[...], TN, preferred_element_type=jnp.float32
        ).astype(jnp.bfloat16)
        low, high = product[:OWNED], product[OWNED:]
        keep_ref[p] = jnp.where(side_ref[1] == 0, low, high)
        send_ref[p] = jnp.where(side_ref[1] == 0, high, low)
    proj_ref[...] = total.astype(jnp.bfloat16)


def main_products(side, own, other, weight, cotangent, gain):
    share = jax.ShapeDtypeStruct((XH * Y, OWNED, COLS), jnp.bfloat16)
    return pl.pallas_call(
        main_kernel,
        out_shape=(jax.ShapeDtypeStruct((GROUP, COLS), jnp.bfloat16), share, share),
        in_specs=[SMEM] + [VMEM] * 5,
        out_specs=(VMEM,) * 3,
        scratch_shapes=[
            pltpu.VMEM((FQ // 128, ROWS, 128), jnp.float32),
            pltpu.VMEM((ROWS, 128), jnp.float32),
        ],
        compiler_params=PARAMS,
        cost_estimate=pl.CostEstimate(
            flops=4 * GROUP * D * COLS, bytes_accessed=12 * 2**20, transcendentals=0
        ),
    )(side, own, other, weight, cotangent, gain)


def exchange(array, axes):
    return lax.all_to_all(array, axes, 0, 0, tiled=True)


def swap(array, axis):
    return lax.ppermute(array, axis, [(0, 1), (1, 0)])


def body(tokens, norm_gain, proj_weight, cotangent):
    side = jnp.stack([lax.axis_index("xl"), lax.axis_index("c")]).astype(jnp.int32)

    comm, grad_keep, grad_send = grad_terms(side, cotangent, proj_weight)
    grad_rows = lax.psum_scatter(comm, "z", scatter_dimension=0, tiled=True)
    grad_got = swap(grad_send, "xl")
    chunk, grad_keep = lax.optimization_barrier((tokens.reshape(TOK * Q, FQ), grad_keep))
    own = lax.all_gather(chunk, "z", axis=0, tiled=True)
    other = swap(own, "xl")

    part = gain_terms(own, grad_keep, grad_got)
    part = jnp.broadcast_to(part.reshape(D // 128, 128), (Y, D // 128, 128))
    part = jnp.sum(exchange(part, "y"), axis=0)
    other, part, grad_rows = lax.optimization_barrier((other, part, grad_rows))
    part = part + swap(part, "c")
    projected, keep, send = main_products(
        side, own, other, proj_weight, cotangent, norm_gain.reshape(1, D)
    )
    share = keep + swap(send, "c")
    share, part = lax.optimization_barrier((share, part))
    weight_grad = jnp.sum(exchange(share, ("xh", "y")).astype(jnp.float32), axis=0)
    part = jnp.sum(lax.all_gather(part, "z"), axis=0)
    part = part + swap(part, "xl")
    gain_grad = (part + swap(part, "xh")).reshape(D)

    values = tokens.astype(jnp.float32)
    rsq = lax.rsqrt(jnp.mean(values * values, axis=-1, keepdims=True) + 1e-05)
    unit_rows = values * rsq
    grad_rows = grad_rows.reshape(XL, TOK, D)
    is_low = side[0] == 0
    grad_rows, moved = (
        jnp.where(is_low, grad_rows[0], grad_rows[1]),
        jnp.where(is_low, grad_rows[1], grad_rows[0]),
    )
    normed_grad = grad_rows.astype(jnp.float32) + swap(moved, "xl").astype(jnp.float32)
    scaled = normed_grad * norm_gain
    input_grad = (
        rsq * (scaled - unit_rows * jnp.mean(scaled * unit_rows, axis=-1, keepdims=True))
    ).astype(jnp.bfloat16)
    return projected, input_grad, weight_grad, gain_grad


def solution(mesh):
    fine = Mesh(mesh.devices.reshape(XH, Y, CORE, XL, Z), AXES)
    return jax.shard_map(
        body,
        mesh=fine,
        in_specs=(P(DP + TENSOR, None), P(), P(None, TENSOR), P(DP, TENSOR)),
        out_specs=(P(DP, TENSOR), P(DP + TENSOR, None), P(DP, TENSOR), P()),
        check_vma=False,
    )
```

```python
import jax
import jax.numpy as jnp
from jax import lax
from jax.experimental import pallas as pl
from jax.experimental.pallas import tpu as pltpu
from jax.sharding import Mesh, PartitionSpec as P

XH, Y, CORE, XL, Z = 2, 8, 2, 2, 12
AXES = ("xh", "y", "c", "xl", "z")
DP, TENSOR = ("xh", "y", "c"), ("xl", "z")
TOK, D, COLS = 6, 6144, 256
Q, FQ = 4, 1536
GROUP = TOK * XL * Z
ROWS = GROUP * Q
HALF = ROWS // 2
CHUNK = TOK * Q
BLOCK = 384
OWNED = BLOCK // 2
NT = (((1,), (1,)), ((), ()))
TN = (((0,), (0,)), ((), ()))
VMEM = pl.BlockSpec(memory_space=pltpu.VMEM)
PARAMS = pltpu.CompilerParams(vmem_limit_bytes=40 * 2**20)
STREAMED = pltpu.CompilerParams(vmem_limit_bytes=60 * 2**20)


def grad_kernel(cot_ref, w_ref, comm_ref, keep_ref, send_ref, wide):
    side = lax.axis_index("xl")
    mine = pl.multiple_of(side * HALF, HALF)
    theirs = pl.multiple_of((1 - side) * HALF, HALF)
    for q in range(Q):
        part = lax.dot_general(cot_ref[...], w_ref[q], NT, preferred_element_type=jnp.float32)
        for b in range(BLOCK // 128):
            wide[b, pl.ds(q, GROUP, stride=Q), :] = part[:, b * 128 : (b + 1) * 128]
    for b in range(BLOCK // 128):
        lanes = slice(b * 128, (b + 1) * 128)
        keep_ref[:, lanes] = wide[b, pl.ds(mine, HALF), :].astype(jnp.bfloat16)
        send_ref[:, lanes] = wide[b, pl.ds(theirs, HALF), :].astype(jnp.bfloat16)
        starts = [x * HALF + z * CHUNK for z in range(Z) for x in range(XL)]
        ordered = jnp.concatenate([wide[b, start : start + CHUNK, :] for start in starts])
        comm_ref[:, lanes] = ordered.astype(jnp.bfloat16)


def grad_terms(cotangent, weight):
    half = jax.ShapeDtypeStruct((HALF, FQ), jnp.bfloat16)
    return pl.pallas_call(
        grad_kernel,
        grid=(FQ // BLOCK,),
        out_shape=(jax.ShapeDtypeStruct((ROWS, FQ), jnp.bfloat16), half, half),
        in_specs=[
            pl.BlockSpec((GROUP, COLS), lambda i: (0, 0)),
            pl.BlockSpec((Q, BLOCK, COLS), lambda i: (0, i, 0)),
        ],
        out_specs=(
            pl.BlockSpec((ROWS, BLOCK), lambda i: (0, i)),
            pl.BlockSpec((HALF, BLOCK), lambda i: (0, i)),
            pl.BlockSpec((HALF, BLOCK), lambda i: (0, i)),
        ),
        scratch_shapes=[pltpu.VMEM((BLOCK // 128, ROWS, 128), jnp.float32)],
        compiler_params=STREAMED,
        cost_estimate=pl.CostEstimate(
            flops=2 * GROUP * D * COLS, bytes_accessed=5 * 2**20, transcendentals=0
        ),
    )(cotangent, weight.reshape(Q, FQ, COLS))


def row_inverse(squares, rows, tokens):
    rows[...] = squares
    total = jnp.zeros((tokens, 128), jnp.float32)
    for q in range(Q):
        total += rows[pl.ds(q, tokens, stride=Q), :]
    return lax.rsqrt(jnp.sum(total, axis=1, keepdims=True) / D + 1e-05)


def gain_kernel(own_ref, keep_ref, got_ref, part_ref, rows):
    squares = jnp.zeros((HALF, 128), jnp.float32)
    for b in range(FQ // 128):
        values = own_ref[:, b * 128 : (b + 1) * 128].astype(jnp.float32)
        squares += values * values
    inverse = row_inverse(squares, rows, GROUP // 2)
    for q in range(Q):
        rows[pl.ds(q, GROUP // 2, stride=Q), :] = jnp.broadcast_to(inverse, (GROUP // 2, 128))
    for b in range(FQ // 128):
        lanes = slice(b * 128, (b + 1) * 128)
        term = keep_ref[:, lanes].astype(jnp.float32) + got_ref[:, lanes].astype(jnp.float32)
        product = own_ref[:, lanes].astype(jnp.float32) * rows[...] * term
        total = jnp.sum(product.reshape(HALF // 8, 8, 128), axis=0)
        part_ref[:, lanes] = total[:Q] + total[Q:]


def gain_terms(own, keep, got):
    return pl.pallas_call(
        gain_kernel,
        out_shape=jax.ShapeDtypeStruct((Q, FQ), jnp.float32),
        in_specs=[VMEM] * 3,
        out_specs=VMEM,
        scratch_shapes=[pltpu.VMEM((HALF, 128), jnp.float32)],
        compiler_params=PARAMS,
        cost_estimate=pl.CostEstimate(flops=5 * 2**20, bytes_accessed=4 * 2**20, transcendentals=0),
    )(own, keep, got)


def main_kernel(
    own_ref, other_ref, cot_ref, gain_ref,
    restored_ref, keep_ref, send_ref, wide, rows,
):
    side = lax.axis_index("xl")
    mine = pl.multiple_of(side * HALF, HALF)
    theirs = pl.multiple_of((1 - side) * HALF, HALF)
    for b in range(FQ // 128):
        wide[b, pl.ds(mine, HALF), :] = own_ref[:, b * 128 : (b + 1) * 128].astype(jnp.float32)
        wide[b, pl.ds(theirs, HALF), :] = other_ref[:, b * 128 : (b + 1) * 128].astype(jnp.float32)
    core = lax.axis_index("c")
    squares = jnp.zeros((ROWS, 128), jnp.float32)
    for b in range(FQ // 128):
        squares += wide[b] * wide[b]
    inverse = row_inverse(squares, rows, GROUP)
    for p in range(D // BLOCK):
        q, first = divmod(p * BLOCK, FQ)
        pieces = []
        for b in range(BLOCK // 128):
            at = p * BLOCK + b * 128
            unit = wide[first // 128 + b, pl.ds(q, GROUP, stride=Q), :] * inverse
            normed = unit * gain_ref[:, at : at + 128]
            scale = (jnp.max(jnp.abs(normed), axis=1, keepdims=True) + 1e-06) / 448.0
            payload = (normed / scale).astype(jnp.bfloat16)
            pieces.append((payload.astype(jnp.float32) * scale).astype(jnp.bfloat16))
        restored = jnp.concatenate(pieces, axis=1)
        restored_ref[:, p * BLOCK : (p + 1) * BLOCK] = restored
        product = lax.dot_general(
            restored, cot_ref[...], TN, preferred_element_type=jnp.float32
        ).astype(jnp.bfloat16)
        low, high = product[:OWNED], product[OWNED:]
        keep_ref[p] = jnp.where(core == 0, low, high)
        send_ref[p] = jnp.where(core == 0, high, low)


def main_products(own, other, cotangent, gain):
    share = jax.ShapeDtypeStruct((XH * Y, OWNED, COLS), jnp.bfloat16)
    return pl.pallas_call(
        main_kernel,
        out_shape=(jax.ShapeDtypeStruct((GROUP, D), jnp.bfloat16), share, share),
        in_specs=[VMEM] * 4,
        out_specs=(VMEM,) * 3,
        scratch_shapes=[
            pltpu.VMEM((FQ // 128, ROWS, 128), jnp.float32),
            pltpu.VMEM((ROWS, 128), jnp.float32),
        ],
        compiler_params=PARAMS,
        cost_estimate=pl.CostEstimate(
            flops=2 * GROUP * D * COLS, bytes_accessed=10 * 2**20, transcendentals=0
        ),
    )(own, other, cotangent, gain)


def exchange(array, axes):
    return lax.all_to_all(array, axes, 0, 0, tiled=True)


def swap(array, axis):
    return lax.ppermute(array, axis, [(0, 1), (1, 0)])


def body(tokens, norm_gain, proj_weight, cotangent):
    comm, grad_keep, grad_send = grad_terms(cotangent, proj_weight)
    grad_rows = lax.psum_scatter(comm, "z", scatter_dimension=0, tiled=True)
    grad_got = swap(grad_send, "xl")
    chunk, grad_keep = lax.optimization_barrier((tokens.reshape(TOK * Q, FQ), grad_keep))
    own = lax.all_gather(chunk, "z", axis=0, tiled=True)
    other = swap(own, "xl")

    part = gain_terms(own, grad_keep, grad_got)
    part = jnp.broadcast_to(part.reshape(D // 128, 128), (Y, D // 128, 128))
    part = jnp.sum(exchange(part, "y"), axis=0)
    other, part = lax.optimization_barrier((other, part))
    part = part + swap(part, "c")
    restored, keep, send = main_products(own, other, cotangent, norm_gain.reshape(1, D))
    share = keep + swap(send, "c")
    projected = jnp.dot(restored, proj_weight, preferred_element_type=jnp.float32)
    projected = projected.astype(jnp.bfloat16)
    share, part, projected, grad_rows = lax.optimization_barrier(
        (share, part, projected, grad_rows)
    )
    weight_grad = jnp.sum(exchange(share, ("xh", "y")).astype(jnp.float32), axis=0)
    part = jnp.sum(lax.all_gather(part, "z"), axis=0)
    part, grad_rows = lax.optimization_barrier((part, grad_rows))
    part = part + swap(part, "xl")
    gain_grad = (part + swap(part, "xh")).reshape(D)

    values = tokens.astype(jnp.float32)
    rsq = lax.rsqrt(jnp.mean(values * values, axis=-1, keepdims=True) + 1e-05)
    unit_rows = values * rsq
    grad_rows = grad_rows.reshape(XL, TOK, D)
    is_low = lax.axis_index("xl") == 0
    grad_rows, moved = (
        jnp.where(is_low, grad_rows[0], grad_rows[1]),
        jnp.where(is_low, grad_rows[1], grad_rows[0]),
    )
    normed_grad = grad_rows.astype(jnp.float32) + swap(moved, "xl").astype(jnp.float32)
    scaled = normed_grad * norm_gain
    input_grad = (
        rsq * (scaled - unit_rows * jnp.mean(scaled * unit_rows, axis=-1, keepdims=True))
    ).astype(jnp.bfloat16)
    return projected, input_grad, weight_grad, gain_grad


def solution(mesh):
    fine = Mesh(mesh.devices.reshape(XH, Y, CORE, XL, Z), AXES)
    return jax.shard_map(
        body,
        mesh=fine,
        in_specs=(P(DP + TENSOR, None), P(), P(None, TENSOR), P(DP, TENSOR)),
        out_specs=(P(DP, TENSOR), P(DP + TENSOR, None), P(DP, TENSOR), P()),
        check_vma=False,
    )
```

```python
import jax
import jax.numpy as jnp
from jax import lax
from jax.experimental import pallas as pl
from jax.experimental.pallas import tpu as pltpu
from jax.sharding import Mesh, PartitionSpec as P

XH, Y, CORE, XL, Z = 2, 8, 2, 2, 12
AXES = ("xh", "y", "c", "xl", "z")
DP, TENSOR = ("xh", "y", "c"), ("xl", "z")
TOK, D, COLS = 6, 6144, 256
Q, FQ = 4, 1536
GROUP = TOK * XL * Z
ROWS = GROUP * Q
HALF = ROWS // 2
CHUNK = TOK * Q
BLOCK = 384
OWNED = BLOCK // 2
NT = (((1,), (1,)), ((), ()))
TN = (((0,), (0,)), ((), ()))
VMEM = pl.BlockSpec(memory_space=pltpu.VMEM)
PARAMS = pltpu.CompilerParams(vmem_limit_bytes=40 * 2**20)
STREAMED = pltpu.CompilerParams(vmem_limit_bytes=60 * 2**20)


def grad_kernel(cot_ref, w_ref, comm_ref, keep_ref, send_ref, wide):
    side = lax.axis_index("xl")
    mine = pl.multiple_of(side * HALF, HALF)
    theirs = pl.multiple_of((1 - side) * HALF, HALF)
    for q in range(Q):
        part = lax.dot_general(cot_ref[...], w_ref[q], NT, preferred_element_type=jnp.float32)
        for b in range(BLOCK // 128):
            wide[b, pl.ds(q, GROUP, stride=Q), :] = part[:, b * 128 : (b + 1) * 128]
    for b in range(BLOCK // 128):
        lanes = slice(b * 128, (b + 1) * 128)
        keep_ref[:, lanes] = wide[b, pl.ds(mine, HALF), :].astype(jnp.bfloat16)
        send_ref[:, lanes] = wide[b, pl.ds(theirs, HALF), :].astype(jnp.bfloat16)
        starts = [x * HALF + z * CHUNK for z in range(Z) for x in range(XL)]
        ordered = jnp.concatenate([wide[b, start : start + CHUNK, :] for start in starts])
        comm_ref[:, lanes] = ordered.astype(jnp.bfloat16)


def grad_terms(cotangent, weight):
    half = jax.ShapeDtypeStruct((HALF, FQ), jnp.bfloat16)
    return pl.pallas_call(
        grad_kernel,
        grid=(FQ // BLOCK,),
        out_shape=(jax.ShapeDtypeStruct((ROWS, FQ), jnp.bfloat16), half, half),
        in_specs=[
            pl.BlockSpec((GROUP, COLS), lambda i: (0, 0)),
            pl.BlockSpec((Q, BLOCK, COLS), lambda i: (0, i, 0)),
        ],
        out_specs=(
            pl.BlockSpec((ROWS, BLOCK), lambda i: (0, i)),
            pl.BlockSpec((HALF, BLOCK), lambda i: (0, i)),
            pl.BlockSpec((HALF, BLOCK), lambda i: (0, i)),
        ),
        scratch_shapes=[pltpu.VMEM((BLOCK // 128, ROWS, 128), jnp.float32)],
        compiler_params=STREAMED,
        cost_estimate=pl.CostEstimate(
            flops=2 * GROUP * D * COLS, bytes_accessed=5 * 2**20, transcendentals=0
        ),
    )(cotangent, weight.reshape(Q, FQ, COLS))


def row_inverse(squares, rows, tokens):
    rows[...] = squares
    total = jnp.zeros((tokens, 128), jnp.float32)
    for q in range(Q):
        total += rows[pl.ds(q, tokens, stride=Q), :]
    return lax.rsqrt(jnp.sum(total, axis=1, keepdims=True) / D + 1e-05)


def gain_kernel(own_ref, keep_ref, got_ref, part_ref, rows):
    squares = jnp.zeros((HALF, 128), jnp.float32)
    for b in range(FQ // 128):
        values = own_ref[:, b * 128 : (b + 1) * 128].astype(jnp.float32)
        squares += values * values
    inverse = row_inverse(squares, rows, GROUP // 2)
    for q in range(Q):
        rows[pl.ds(q, GROUP // 2, stride=Q), :] = jnp.broadcast_to(inverse, (GROUP // 2, 128))
    for b in range(FQ // 128):
        lanes = slice(b * 128, (b + 1) * 128)
        term = keep_ref[:, lanes].astype(jnp.float32) + got_ref[:, lanes].astype(jnp.float32)
        product = own_ref[:, lanes].astype(jnp.float32) * rows[...] * term
        total = jnp.sum(product.reshape(HALF // 8, 8, 128), axis=0)
        total = total[:Q] + total[Q:]
        for q in range(Q):
            row = q * (FQ // 128) + b
            part_ref[:, row : row + 1, :] = jnp.broadcast_to(total[q : q + 1], (Y, 1, 128))


def gain_terms(own, keep, got):
    return pl.pallas_call(
        gain_kernel,
        out_shape=jax.ShapeDtypeStruct((Y, D // 128, 128), jnp.float32),
        in_specs=[VMEM] * 3,
        out_specs=VMEM,
        scratch_shapes=[pltpu.VMEM((HALF, 128), jnp.float32)],
        compiler_params=PARAMS,
        cost_estimate=pl.CostEstimate(flops=5 * 2**20, bytes_accessed=4 * 2**20, transcendentals=0),
    )(own, keep, got)


def main_kernel(
    own_ref, other_ref, cot_ref, gain_ref,
    restored_ref, keep_ref, send_ref, wide, rows,
):
    side = lax.axis_index("xl")
    mine = pl.multiple_of(side * HALF, HALF)
    theirs = pl.multiple_of((1 - side) * HALF, HALF)
    for b in range(FQ // 128):
        wide[b, pl.ds(mine, HALF), :] = own_ref[:, b * 128 : (b + 1) * 128].astype(jnp.float32)
        wide[b, pl.ds(theirs, HALF), :] = other_ref[:, b * 128 : (b + 1) * 128].astype(jnp.float32)
    core = lax.axis_index("c")
    squares = jnp.zeros((ROWS, 128), jnp.float32)
    for b in range(FQ // 128):
        squares += wide[b] * wide[b]
    inverse = row_inverse(squares, rows, GROUP)
    for p in range(D // BLOCK):
        q, first = divmod(p * BLOCK, FQ)
        pieces = []
        for b in range(BLOCK // 128):
            at = p * BLOCK + b * 128
            unit = wide[first // 128 + b, pl.ds(q, GROUP, stride=Q), :] * inverse
            normed = unit * gain_ref[:, at : at + 128]
            scale = (jnp.max(jnp.abs(normed), axis=1, keepdims=True) + 1e-06) / 448.0
            payload = (normed / scale).astype(jnp.bfloat16)
            pieces.append((payload.astype(jnp.float32) * scale).astype(jnp.bfloat16))
        restored = jnp.concatenate(pieces, axis=1)
        restored_ref[:, p * BLOCK : (p + 1) * BLOCK] = restored
        product = lax.dot_general(
            restored, cot_ref[...], TN, preferred_element_type=jnp.float32
        ).astype(jnp.bfloat16)
        low, high = product[:OWNED], product[OWNED:]
        keep_ref[p] = jnp.where(core == 0, low, high)
        send_ref[p] = jnp.where(core == 0, high, low)


def main_products(own, other, cotangent, gain):
    share = jax.ShapeDtypeStruct((XH * Y, OWNED, COLS), jnp.bfloat16)
    return pl.pallas_call(
        main_kernel,
        out_shape=(jax.ShapeDtypeStruct((GROUP, D), jnp.bfloat16), share, share),
        in_specs=[VMEM] * 4,
        out_specs=(VMEM,) * 3,
        scratch_shapes=[
            pltpu.VMEM((FQ // 128, ROWS, 128), jnp.float32),
            pltpu.VMEM((ROWS, 128), jnp.float32),
        ],
        compiler_params=PARAMS,
        cost_estimate=pl.CostEstimate(
            flops=2 * GROUP * D * COLS, bytes_accessed=10 * 2**20, transcendentals=0
        ),
    )(own, other, cotangent, gain)


def exchange(array, axes):
    return lax.all_to_all(array, axes, 0, 0, tiled=True)


def swap(array, axis):
    return lax.ppermute(array, axis, [(0, 1), (1, 0)])


def body(tokens, norm_gain, proj_weight, cotangent):
    comm, grad_keep, grad_send = grad_terms(cotangent, proj_weight)
    grad_rows = lax.psum_scatter(comm, "z", scatter_dimension=0, tiled=True)
    grad_got = swap(grad_send, "xl")
    chunk, grad_keep = lax.optimization_barrier((tokens.reshape(TOK * Q, FQ), grad_keep))
    own = lax.all_gather(chunk, "z", axis=0, tiled=True)
    other = swap(own, "xl")

    part = gain_terms(own, grad_keep, grad_got)
    part = jnp.sum(exchange(part, "y"), axis=0)
    other, part = lax.optimization_barrier((other, part))
    part = part + swap(part, "c")
    restored, keep, send = main_products(own, other, cotangent, norm_gain.reshape(1, D))
    share = keep + swap(send, "c")
    projected = jnp.dot(restored, proj_weight, preferred_element_type=jnp.float32)
    projected = projected.astype(jnp.bfloat16)
    share, part, projected, grad_rows = lax.optimization_barrier(
        (share, part, projected, grad_rows)
    )
    weight_grad = jnp.sum(exchange(share, ("xh", "y")).astype(jnp.float32), axis=0)
    part = jnp.sum(lax.all_gather(part, "z"), axis=0)
    part, grad_rows = lax.optimization_barrier((part, grad_rows))
    part = part + swap(part, "xl")
    gain_grad = (part + swap(part, "xh")).reshape(D)

    values = tokens.astype(jnp.float32)
    rsq = lax.rsqrt(jnp.mean(values * values, axis=-1, keepdims=True) + 1e-05)
    unit_rows = values * rsq
    grad_rows = grad_rows.reshape(XL, TOK, D)
    is_low = lax.axis_index("xl") == 0
    grad_rows, moved = (
        jnp.where(is_low, grad_rows[0], grad_rows[1]),
        jnp.where(is_low, grad_rows[1], grad_rows[0]),
    )
    normed_grad = grad_rows.astype(jnp.float32) + swap(moved, "xl").astype(jnp.float32)
    scaled = normed_grad * norm_gain
    input_grad = (
        rsq * (scaled - unit_rows * jnp.mean(scaled * unit_rows, axis=-1, keepdims=True))
    ).astype(jnp.bfloat16)
    return projected, input_grad, weight_grad, gain_grad


def solution(mesh):
    fine = Mesh(mesh.devices.reshape(XH, Y, CORE, XL, Z), AXES)
    return jax.shard_map(
        body,
        mesh=fine,
        in_specs=(P(DP + TENSOR, None), P(), P(None, TENSOR), P(DP, TENSOR)),
        out_specs=(P(DP, TENSOR), P(DP + TENSOR, None), P(DP, TENSOR), P()),
        check_vma=False,
    )
```

```python
import jax
import jax.numpy as jnp
from jax import lax
from jax.experimental import pallas as pl
from jax.experimental.pallas import tpu as pltpu
from jax.sharding import Mesh, PartitionSpec as P

XH, Y, CORE, XL, Z = 2, 8, 2, 2, 12
AXES = ("xh", "y", "c", "xl", "z")
DP, TENSOR = ("xh", "y", "c"), ("xl", "z")
TOK, D, COLS = 6, 6144, 256
Q, FQ = 4, 1536
GROUP = TOK * XL * Z
ROWS = GROUP * Q
HALF = ROWS // 2
CHUNK = TOK * Q
BLOCK = 384
OWNED = BLOCK // 2
NT = (((1,), (1,)), ((), ()))
TN = (((0,), (0,)), ((), ()))
VMEM = pl.BlockSpec(memory_space=pltpu.VMEM)
PARAMS = pltpu.CompilerParams(vmem_limit_bytes=40 * 2**20)
STREAMED = pltpu.CompilerParams(vmem_limit_bytes=60 * 2**20)


def grad_kernel(cot_ref, w_ref, comm_ref, keep_ref, send_ref, wide):
    side = lax.axis_index("xl")
    mine = pl.multiple_of(side * HALF, HALF)
    theirs = pl.multiple_of((1 - side) * HALF, HALF)
    for q in range(Q):
        part = lax.dot_general(cot_ref[...], w_ref[q], NT, preferred_element_type=jnp.float32)
        for b in range(BLOCK // 128):
            wide[b, pl.ds(q, GROUP, stride=Q), :] = part[:, b * 128 : (b + 1) * 128]
    for b in range(BLOCK // 128):
        lanes = slice(b * 128, (b + 1) * 128)
        keep_ref[:, lanes] = wide[b, pl.ds(mine, HALF), :].astype(jnp.bfloat16)
        send_ref[:, lanes] = wide[b, pl.ds(theirs, HALF), :].astype(jnp.bfloat16)
        starts = [x * HALF + z * CHUNK for z in range(Z) for x in range(XL)]
        ordered = jnp.concatenate([wide[b, start : start + CHUNK, :] for start in starts])
        comm_ref[:, lanes] = ordered.astype(jnp.bfloat16)


def grad_terms(cotangent, weight):
    half = jax.ShapeDtypeStruct((HALF, FQ), jnp.bfloat16)
    return pl.pallas_call(
        grad_kernel,
        grid=(FQ // BLOCK,),
        out_shape=(jax.ShapeDtypeStruct((ROWS, FQ), jnp.bfloat16), half, half),
        in_specs=[
            pl.BlockSpec((GROUP, COLS), lambda i: (0, 0)),
            pl.BlockSpec((Q, BLOCK, COLS), lambda i: (0, i, 0)),
        ],
        out_specs=(
            pl.BlockSpec((ROWS, BLOCK), lambda i: (0, i)),
            pl.BlockSpec((HALF, BLOCK), lambda i: (0, i)),
            pl.BlockSpec((HALF, BLOCK), lambda i: (0, i)),
        ),
        scratch_shapes=[pltpu.VMEM((BLOCK // 128, ROWS, 128), jnp.float32)],
        compiler_params=STREAMED,
        cost_estimate=pl.CostEstimate(
            flops=2 * GROUP * D * COLS, bytes_accessed=5 * 2**20, transcendentals=0
        ),
    )(cotangent, weight.reshape(Q, FQ, COLS))


def row_inverse(squares, rows, tokens):
    rows[...] = squares
    total = jnp.zeros((tokens, 128), jnp.float32)
    for q in range(Q):
        total += rows[pl.ds(q, tokens, stride=Q), :]
    return lax.rsqrt(jnp.sum(total, axis=1, keepdims=True) / D + 1e-05)


def gain_kernel(own_ref, keep_ref, got_ref, part_ref, rows):
    squares = jnp.zeros((HALF, 128), jnp.float32)
    for b in range(FQ // 128):
        values = own_ref[:, b * 128 : (b + 1) * 128].astype(jnp.float32)
        squares += values * values
    inverse = row_inverse(squares, rows, GROUP // 2)
    for q in range(Q):
        rows[pl.ds(q, GROUP // 2, stride=Q), :] = jnp.broadcast_to(inverse, (GROUP // 2, 128))
    for b in range(FQ // 128):
        lanes = slice(b * 128, (b + 1) * 128)
        term = keep_ref[:, lanes].astype(jnp.float32) + got_ref[:, lanes].astype(jnp.float32)
        product = own_ref[:, lanes].astype(jnp.float32) * rows[...] * term
        total = jnp.sum(product.reshape(HALF // 8, 8, 128), axis=0)
        total = total[:Q] + total[Q:]
        for q in range(Q):
            row = q * (FQ // 128) + b
            part_ref[:, row : row + 1, :] = jnp.broadcast_to(total[q : q + 1], (Y, 1, 128))


def gain_terms(own, keep, got):
    return pl.pallas_call(
        gain_kernel,
        out_shape=jax.ShapeDtypeStruct((Y, D // 128, 128), jnp.float32),
        in_specs=[VMEM] * 3,
        out_specs=VMEM,
        scratch_shapes=[pltpu.VMEM((HALF, 128), jnp.float32)],
        compiler_params=PARAMS,
        cost_estimate=pl.CostEstimate(flops=5 * 2**20, bytes_accessed=4 * 2**20, transcendentals=0),
    )(own, keep, got)


def main_kernel(
    own_ref, other_ref, cot_ref, gain_ref,
    restored_ref, keep_ref, send_ref, wide, rows,
):
    side = lax.axis_index("xl")
    mine = pl.multiple_of(side * HALF, HALF)
    theirs = pl.multiple_of((1 - side) * HALF, HALF)
    for b in range(FQ // 128):
        wide[b, pl.ds(mine, HALF), :] = own_ref[:, b * 128 : (b + 1) * 128].astype(jnp.float32)
        wide[b, pl.ds(theirs, HALF), :] = other_ref[:, b * 128 : (b + 1) * 128].astype(jnp.float32)
    core = lax.axis_index("c")
    squares = jnp.zeros((ROWS, 128), jnp.float32)
    for b in range(FQ // 128):
        squares += wide[b] * wide[b]
    inverse = row_inverse(squares, rows, GROUP)
    for p in range(D // BLOCK):
        q, first = divmod(p * BLOCK, FQ)
        pieces = []
        for b in range(BLOCK // 128):
            at = p * BLOCK + b * 128
            unit = wide[first // 128 + b, pl.ds(q, GROUP, stride=Q), :] * inverse
            normed = unit * gain_ref[:, at : at + 128]
            scale = (jnp.max(jnp.abs(normed), axis=1, keepdims=True) + 1e-06) / 448.0
            payload = (normed / scale).astype(jnp.bfloat16)
            pieces.append((payload.astype(jnp.float32) * scale).astype(jnp.bfloat16))
        restored = jnp.concatenate(pieces, axis=1)
        restored_ref[:, p * BLOCK : (p + 1) * BLOCK] = restored
        product = lax.dot_general(
            restored, cot_ref[...], TN, preferred_element_type=jnp.float32
        ).astype(jnp.bfloat16)
        low, high = product[:OWNED], product[OWNED:]
        keep_ref[p] = jnp.where(core == 0, low, high)
        send_ref[p] = jnp.where(core == 0, high, low)


def main_products(own, other, cotangent, gain):
    share = jax.ShapeDtypeStruct((XH * Y, OWNED, COLS), jnp.bfloat16)
    return pl.pallas_call(
        main_kernel,
        out_shape=(jax.ShapeDtypeStruct((GROUP, D), jnp.bfloat16), share, share),
        in_specs=[VMEM] * 4,
        out_specs=(VMEM,) * 3,
        scratch_shapes=[
            pltpu.VMEM((FQ // 128, ROWS, 128), jnp.float32),
            pltpu.VMEM((ROWS, 128), jnp.float32),
        ],
        compiler_params=PARAMS,
        cost_estimate=pl.CostEstimate(
            flops=2 * GROUP * D * COLS, bytes_accessed=10 * 2**20, transcendentals=0
        ),
    )(own, other, cotangent, gain)


def exchange(array, axes):
    return lax.all_to_all(array, axes, 0, 0, tiled=True)


def swap(array, axis):
    return lax.ppermute(array, axis, [(0, 1), (1, 0)])


def body(tokens, norm_gain, proj_weight, cotangent):
    comm, grad_keep, grad_send = grad_terms(cotangent, proj_weight)
    grad_rows = lax.psum_scatter(comm, "z", scatter_dimension=0, tiled=True)
    grad_got = swap(grad_send, "xl")
    chunk, grad_keep = lax.optimization_barrier((tokens.reshape(TOK * Q, FQ), grad_keep))
    own = lax.all_gather(chunk, "z", axis=0, tiled=True)
    other = swap(own, "xl")

    part = gain_terms(own, grad_keep, grad_got)
    part = jnp.sum(exchange(part, "y"), axis=0)
    other, part = lax.optimization_barrier((other, part))
    part = part + swap(part, "xh")
    restored, keep, send = main_products(own, other, cotangent, norm_gain.reshape(1, D))
    share = keep + swap(send, "c")
    projected = jnp.dot(restored, proj_weight, preferred_element_type=jnp.float32)
    projected = projected.astype(jnp.bfloat16)
    share, part, projected, grad_rows = lax.optimization_barrier(
        (share, part, projected, grad_rows)
    )
    weight_grad = jnp.sum(exchange(share, ("xh", "y")).astype(jnp.float32), axis=0)
    part = jnp.sum(lax.all_gather(part, "z"), axis=0)
    part, grad_rows = lax.optimization_barrier((part, grad_rows))
    part = part + swap(part, "xl")
    gain_grad = (part + swap(part, "c")).reshape(D)

    values = tokens.astype(jnp.float32)
    rsq = lax.rsqrt(jnp.mean(values * values, axis=-1, keepdims=True) + 1e-05)
    unit_rows = values * rsq
    grad_rows = grad_rows.reshape(XL, TOK, D)
    is_low = lax.axis_index("xl") == 0
    grad_rows, moved = (
        jnp.where(is_low, grad_rows[0], grad_rows[1]),
        jnp.where(is_low, grad_rows[1], grad_rows[0]),
    )
    normed_grad = grad_rows.astype(jnp.float32) + swap(moved, "xl").astype(jnp.float32)
    scaled = normed_grad * norm_gain
    input_grad = (
        rsq * (scaled - unit_rows * jnp.mean(scaled * unit_rows, axis=-1, keepdims=True))
    ).astype(jnp.bfloat16)
    return projected, input_grad, weight_grad, gain_grad


def solution(mesh):
    fine = Mesh(mesh.devices.reshape(XH, Y, CORE, XL, Z), AXES)
    return jax.shard_map(
        body,
        mesh=fine,
        in_specs=(P(DP + TENSOR, None), P(), P(None, TENSOR), P(DP, TENSOR)),
        out_specs=(P(DP, TENSOR), P(DP + TENSOR, None), P(DP, TENSOR), P()),
        check_vma=False,
    )
```

```python
import jax
import jax.numpy as jnp
from jax import lax
from jax.experimental import pallas as pl
from jax.experimental.pallas import tpu as pltpu
from jax.sharding import Mesh, PartitionSpec as P

XH, Y, CORE, XL, Z = 2, 8, 2, 2, 12
AXES = ("xh", "y", "c", "xl", "z")
DP, TENSOR = ("xh", "y", "c"), ("xl", "z")
TOK, D, COLS = 6, 6144, 256
Q, FQ = 4, 1536
GROUP = TOK * XL * Z
ROWS = GROUP * Q
HALF = ROWS // 2
CHUNK = TOK * Q
BLOCK = 384
STEP = 256
OWNED = BLOCK // 2
NT = (((1,), (1,)), ((), ()))
TN = (((0,), (0,)), ((), ()))
VMEM = pl.BlockSpec(memory_space=pltpu.VMEM)
PARAMS = pltpu.CompilerParams(vmem_limit_bytes=40 * 2**20)
STREAMED = pltpu.CompilerParams(vmem_limit_bytes=60 * 2**20)


def grad_kernel(cot_ref, w_ref, comm_ref, keep_ref, send_ref, wide):
    side = lax.axis_index("xl")
    mine = pl.multiple_of(side * HALF, HALF)
    theirs = pl.multiple_of((1 - side) * HALF, HALF)
    for q in range(Q):
        part = lax.dot_general(cot_ref[...], w_ref[q], NT, preferred_element_type=jnp.float32)
        for b in range(STEP // 128):
            wide[b, pl.ds(q, GROUP, stride=Q), :] = part[:, b * 128 : (b + 1) * 128]
    for b in range(STEP // 128):
        lanes = slice(b * 128, (b + 1) * 128)
        keep_ref[:, lanes] = wide[b, pl.ds(mine, HALF), :].astype(jnp.bfloat16)
        send_ref[:, lanes] = wide[b, pl.ds(theirs, HALF), :].astype(jnp.bfloat16)
        starts = [x * HALF + z * CHUNK for z in range(Z) for x in range(XL)]
        ordered = jnp.concatenate([wide[b, start : start + CHUNK, :] for start in starts])
        comm_ref[:, lanes] = ordered.astype(jnp.bfloat16)


def grad_terms(cotangent, weight):
    half = jax.ShapeDtypeStruct((HALF, FQ), jnp.bfloat16)
    return pl.pallas_call(
        grad_kernel,
        grid=(FQ // STEP,),
        out_shape=(jax.ShapeDtypeStruct((ROWS, FQ), jnp.bfloat16), half, half),
        in_specs=[
            pl.BlockSpec((GROUP, COLS), lambda i: (0, 0)),
            pl.BlockSpec((Q, STEP, COLS), lambda i: (0, i, 0)),
        ],
        out_specs=(
            pl.BlockSpec((ROWS, STEP), lambda i: (0, i)),
            pl.BlockSpec((HALF, STEP), lambda i: (0, i)),
            pl.BlockSpec((HALF, STEP), lambda i: (0, i)),
        ),
        scratch_shapes=[pltpu.VMEM((STEP // 128, ROWS, 128), jnp.float32)],
        compiler_params=STREAMED,
        cost_estimate=pl.CostEstimate(
            flops=2 * GROUP * D * COLS, bytes_accessed=5 * 2**20, transcendentals=0
        ),
    )(cotangent, weight.reshape(Q, FQ, COLS))


def row_inverse(squares, rows, tokens):
    rows[...] = squares
    total = jnp.zeros((tokens, 128), jnp.float32)
    for q in range(Q):
        total += rows[pl.ds(q, tokens, stride=Q), :]
    return lax.rsqrt(jnp.sum(total, axis=1, keepdims=True) / D + 1e-05)


def gain_kernel(own_ref, keep_ref, got_ref, part_ref, rows):
    squares = jnp.zeros((HALF, 128), jnp.float32)
    for b in range(FQ // 128):
        values = own_ref[:, b * 128 : (b + 1) * 128].astype(jnp.float32)
        squares += values * values
    inverse = row_inverse(squares, rows, GROUP // 2)
    for q in range(Q):
        rows[pl.ds(q, GROUP // 2, stride=Q), :] = jnp.broadcast_to(inverse, (GROUP // 2, 128))
    for b in range(FQ // 128):
        lanes = slice(b * 128, (b + 1) * 128)
        term = keep_ref[:, lanes].astype(jnp.float32) + got_ref[:, lanes].astype(jnp.float32)
        product = own_ref[:, lanes].astype(jnp.float32) * rows[...] * term
        total = jnp.sum(product.reshape(HALF // 8, 8, 128), axis=0)
        total = total[:Q] + total[Q:]
        for q in range(Q):
            row = q * (FQ // 128) + b
            part_ref[:, row : row + 1, :] = jnp.broadcast_to(total[q : q + 1], (Y, 1, 128))


def gain_terms(own, keep, got):
    return pl.pallas_call(
        gain_kernel,
        out_shape=jax.ShapeDtypeStruct((Y, D // 128, 128), jnp.float32),
        in_specs=[VMEM] * 3,
        out_specs=VMEM,
        scratch_shapes=[pltpu.VMEM((HALF, 128), jnp.float32)],
        compiler_params=PARAMS,
        cost_estimate=pl.CostEstimate(flops=5 * 2**20, bytes_accessed=4 * 2**20, transcendentals=0),
    )(own, keep, got)


def main_kernel(
    own_ref, other_ref, cot_ref, gain_ref,
    restored_ref, keep_ref, send_ref, wide, rows,
):
    side = lax.axis_index("xl")
    mine = pl.multiple_of(side * HALF, HALF)
    theirs = pl.multiple_of((1 - side) * HALF, HALF)
    for b in range(FQ // 128):
        wide[b, pl.ds(mine, HALF), :] = own_ref[:, b * 128 : (b + 1) * 128].astype(jnp.float32)
        wide[b, pl.ds(theirs, HALF), :] = other_ref[:, b * 128 : (b + 1) * 128].astype(jnp.float32)
    core = lax.axis_index("c")
    squares = jnp.zeros((ROWS, 128), jnp.float32)
    for b in range(FQ // 128):
        squares += wide[b] * wide[b]
    inverse = row_inverse(squares, rows, GROUP)
    for p in range(D // BLOCK):
        q, first = divmod(p * BLOCK, FQ)
        pieces = []
        for b in range(BLOCK // 128):
            at = p * BLOCK + b * 128
            unit = wide[first // 128 + b, pl.ds(q, GROUP, stride=Q), :] * inverse
            normed = unit * gain_ref[:, at : at + 128]
            scale = (jnp.max(jnp.abs(normed), axis=1, keepdims=True) + 1e-06) / 448.0
            payload = (normed / scale).astype(jnp.bfloat16)
            pieces.append((payload.astype(jnp.float32) * scale).astype(jnp.bfloat16))
        restored = jnp.concatenate(pieces, axis=1)
        restored_ref[:, p * BLOCK : (p + 1) * BLOCK] = restored
        product = lax.dot_general(
            restored, cot_ref[...], TN, preferred_element_type=jnp.float32
        ).astype(jnp.bfloat16)
        low, high = product[:OWNED], product[OWNED:]
        keep_ref[p] = jnp.where(core == 0, low, high)
        send_ref[p] = jnp.where(core == 0, high, low)


def main_products(own, other, cotangent, gain):
    share = jax.ShapeDtypeStruct((XH * Y, OWNED, COLS), jnp.bfloat16)
    return pl.pallas_call(
        main_kernel,
        out_shape=(jax.ShapeDtypeStruct((GROUP, D), jnp.bfloat16), share, share),
        in_specs=[VMEM] * 4,
        out_specs=(VMEM,) * 3,
        scratch_shapes=[
            pltpu.VMEM((FQ // 128, ROWS, 128), jnp.float32),
            pltpu.VMEM((ROWS, 128), jnp.float32),
        ],
        compiler_params=PARAMS,
        cost_estimate=pl.CostEstimate(
            flops=2 * GROUP * D * COLS, bytes_accessed=10 * 2**20, transcendentals=0
        ),
    )(own, other, cotangent, gain)


def exchange(array, axes):
    return lax.all_to_all(array, axes, 0, 0, tiled=True)


def swap(array, axis):
    return lax.ppermute(array, axis, [(0, 1), (1, 0)])


def body(tokens, norm_gain, proj_weight, cotangent):
    comm, grad_keep, grad_send = grad_terms(cotangent, proj_weight)
    grad_rows = lax.psum_scatter(comm, "z", scatter_dimension=0, tiled=True)
    grad_got = swap(grad_send, "xl")
    chunk, grad_keep = lax.optimization_barrier((tokens.reshape(TOK * Q, FQ), grad_keep))
    own = lax.all_gather(chunk, "z", axis=0, tiled=True)
    other = swap(own, "xl")

    part = gain_terms(own, grad_keep, grad_got)
    part = jnp.sum(exchange(part, "y"), axis=0)
    other, part = lax.optimization_barrier((other, part))
    part = part + swap(part, "xh")
    restored, keep, send = main_products(own, other, cotangent, norm_gain.reshape(1, D))
    share = keep + swap(send, "c")
    projected = jnp.dot(restored, proj_weight, preferred_element_type=jnp.float32)
    projected = projected.astype(jnp.bfloat16)
    share, part, projected, grad_rows = lax.optimization_barrier(
        (share, part, projected, grad_rows)
    )
    weight_grad = jnp.sum(exchange(share, ("xh", "y")).astype(jnp.float32), axis=0)
    part = jnp.sum(lax.all_gather(part, "z"), axis=0)
    part, grad_rows = lax.optimization_barrier((part, grad_rows))
    part = part + swap(part, "xl")
    gain_grad = (part + swap(part, "c")).reshape(D)

    values = tokens.astype(jnp.float32)
    rsq = lax.rsqrt(jnp.mean(values * values, axis=-1, keepdims=True) + 1e-05)
    unit_rows = values * rsq
    grad_rows = grad_rows.reshape(XL, TOK, D)
    is_low = lax.axis_index("xl") == 0
    grad_rows, moved = (
        jnp.where(is_low, grad_rows[0], grad_rows[1]),
        jnp.where(is_low, grad_rows[1], grad_rows[0]),
    )
    normed_grad = grad_rows.astype(jnp.float32) + swap(moved, "xl").astype(jnp.float32)
    scaled = normed_grad * norm_gain
    input_grad = (
        rsq * (scaled - unit_rows * jnp.mean(scaled * unit_rows, axis=-1, keepdims=True))
    ).astype(jnp.bfloat16)
    return projected, input_grad, weight_grad, gain_grad


def solution(mesh):
    fine = Mesh(mesh.devices.reshape(XH, Y, CORE, XL, Z), AXES)
    return jax.shard_map(
        body,
        mesh=fine,
        in_specs=(P(DP + TENSOR, None), P(), P(None, TENSOR), P(DP, TENSOR)),
        out_specs=(P(DP, TENSOR), P(DP + TENSOR, None), P(DP, TENSOR), P()),
        check_vma=False,
    )
```
